32 devices in a mesh: lat: 4 (over z), lon: 8 (over y, x, core).
Axes of the slice: x: 2, y: 2, z: 4, core: 2. Of those that a mesh axis runs over, the one named last changes fastest.
Arguments:
- tokens: bfloat16 [8, 12, 128, 384], P(None, 'lat', 'lon'), may hold values from -6 to 6
- gain_attn: float32 [384], replicated, may hold values from 0.25 to 1.75
- w_qkv: bfloat16 [384, 1152], replicated, may hold values from -0.3125 to 0.3125
- esb: float32 [12, 12, 5], P('lat'), may hold values from -4 to 250
- w_out: bfloat16 [384, 384], replicated, may hold values from -0.3125 to 0.3125
- gain_mlp: float32 [384], replicated, may hold values from 0.25 to 1.75
- w_up: bfloat16 [384, 1536], replicated, may hold values from -0.3125 to 0.3125
- w_down: bfloat16 [1536, 384], replicated, may hold values from -0.15625 to 0.15625
- widths: int32 [4], replicated, may hold values from 1 to 8, as said below
- shifts: int32 [4], replicated, may hold values from 0 to 7
Outputs:
- result: bfloat16 [8, 12, 128, 384], P(None, 'lat', 'lon')
The draws below stay inside these ranges and needn't reach their ends.
Inputs may be any that keep to these rules, and one draw needn't show every extreme that they name: `widths`: each width is a power of two; some band has 8 (the whole circle) and some band has 1.
All inputs are finite; a program needn't handle non-finite values.
Results may differ from the reference program's by a relative error of at most 0.011.
Values may be sent and summed in bfloat16 or wider, within the bound.
A program may use at most 704 MiB of HBM per device.

```python
import jax
import jax.numpy as jnp
import numpy as np
from jax import lax

C = 384
HEADS = 12
FF = 1536
LEVELS = 8
ROWS = 3
COLS = 16
RIM = 1
EXT = 5
WMAX = 8
LAT_BANDS = 4
LATS = 12
LONS = 128
N_LON = 8


def draw_esb(key, part):
    key = jax.random.fold_in(key, 7)
    first = jax.random.fold_in(key, 0)
    return jnp.clip(jax.random.normal(first, (LATS, HEADS, EXT), jnp.float32), -4.0, 4.0)


def draw_widths(key, part):
    key = jax.random.fold_in(key, 3)
    first, second = jax.random.split(key, 2)
    table = jnp.array(np.array([2 ** k for k in range(8) if 2 ** k <= WMAX], dtype=np.int32))
    picks = jax.random.randint(first, (LAT_BANDS,), 0, table.shape[0])
    chosen = table[picks]
    order = jax.random.permutation(second, LAT_BANDS)
    chosen = chosen.at[order[0]].set(WMAX).at[order[1]].set(1)
    return chosen.astype(jnp.int32)


def set_ends(values, rng, low, high):
    extent = values.shape
    place = [jax.random.randint(jax.random.fold_in(rng, axis), (), 0, extent[axis]) for axis in range(len(extent))]
    values = values.at[tuple(place)].set(low)
    longest = extent.index(max(extent))
    place[longest] = (place[longest] + 1) % extent[longest]
    return values.at[tuple(place)].set(high)


def block_levels(stream_key, shape, cuts, smallest, largest):
    level = 1.0
    for axis_at, parts in cuts:
        steps = jax.random.uniform(jax.random.fold_in(jax.random.fold_in(stream_key, 6), axis_at), (parts,), jnp.float32, smallest / len(cuts), largest / len(cuts))
        level = level * jnp.repeat(jnp.exp(steps), shape[axis_at] // parts).reshape((-1,) + (1,) * (len(shape) - 1 - axis_at))
    return level


def normal_values(stream_key, dims, deviation, limit, cuts=(), kind=jnp.bfloat16):
    level = block_levels(stream_key, dims, cuts, -0.22, 0.18) if cuts else 1.0
    entries = jax.random.normal(stream_key, dims, jnp.float32) * deviation * level
    return jnp.minimum(jnp.maximum(entries, -limit), limit).astype(kind)


def setup_inputs(seed: int = 0) -> dict:
    splits = jax.random.split(jax.random.key(seed), 11)
    return {
        "tokens": normal_values(splits[0], (LEVELS, LATS, LONS, C), 1.0, 6.0, ((1, 4), (2, 8))),
        "gain_attn": jnp.clip(1.0 + 0.15 * jax.random.normal(splits[1], (C,), jnp.float32), 0.25, 1.75),
        "w_qkv": normal_values(splits[2], (C, 3 * C), C ** -0.5, 0.3125),
        "esb": draw_esb(jax.random.fold_in(splits[10], 71), 0),
        "w_out": normal_values(splits[4], (C, C), C ** -0.5, 0.3125),
        "gain_mlp": jnp.clip(1.0 + 0.15 * jax.random.normal(splits[5], (C,), jnp.float32), 0.25, 1.75),
        "w_up": normal_values(splits[6], (C, FF), C ** -0.5, 0.3125),
        "w_down": normal_values(splits[7], (FF, C), FF ** -0.5, 0.15625),
        "widths": draw_widths(jax.random.fold_in(splits[10], 71), 0),
        "shifts": set_ends(jax.random.randint(splits[9], (LAT_BANDS,), 0, N_LON), jax.random.fold_in(splits[9], 1), 0, N_LON - 1).astype(jnp.int32),
    }


EPS = 1e-05
NEG = -1e+30

def normalize(rows, gain):
    mean = lax.optimization_barrier(jnp.mean(rows, axis=-1, keepdims=True))
    centred = rows - mean
    spread = lax.optimization_barrier(jnp.mean(centred * centred, axis=-1, keepdims=True))
    return centred * lax.rsqrt(spread + EPS) * gain.astype(jnp.float32)

def attend(q_blk, k_blk, bias, rows_ok, cols_ok):
    lev, rows, cols, width = q_blk.shape
    ext, kcols = (k_blk.shape[1], k_blk.shape[2])
    dim = width // HEADS
    queries = q_blk.reshape(-1, HEADS, dim).transpose(1, 0, 2)
    keys = k_blk[..., :width].reshape(-1, HEADS, dim).transpose(1, 0, 2)
    values = k_blk[..., width:].reshape(-1, HEADS, dim).transpose(1, 0, 2)
    bias_q = jnp.broadcast_to(bias.astype(jnp.float32)[None, :, None], (lev, rows, cols, HEADS, ext))
    bias_q = bias_q.reshape(-1, HEADS, ext).transpose(1, 0, 2)
    valid = rows_ok[:, None] & cols_ok[None, :]
    valid_flat = jnp.broadcast_to(valid[None], (lev, ext, kcols)).reshape(-1)
    scale = dim ** (-0.5)

    def per_head(args):
        q_h, b_h, k_h, v_h = args
        scores = jnp.dot(q_h, k_h.T, preferred_element_type=jnp.float32) * scale
        scores = scores.reshape(-1, lev, ext, kcols) + b_h[:, None, :, None]
        scores = scores.reshape(scores.shape[0], -1)
        scores = jnp.where(valid_flat[None, :], scores, NEG)
        top = lax.optimization_barrier(jnp.max(scores, axis=1, keepdims=True))
        weights = jnp.where(valid_flat[None, :], jnp.exp(scores - top), 0.0)
        total = lax.optimization_barrier(jnp.sum(weights, axis=1, keepdims=True))
        mixed = jnp.dot(weights.astype(jnp.bfloat16), v_h, preferred_element_type=jnp.float32)
        return mixed / total
    out = lax.map(per_head, (queries, bias_q, keys, values))
    return out.transpose(1, 0, 2).reshape(-1, width)

def reference(tokens, gain_attn, w_qkv, esb, w_out, gain_mlp, w_up, w_down, widths, shifts):
    width = tokens.shape[-1]
    flat = tokens.reshape(-1, width).astype(jnp.float32)
    h_one = normalize(flat, gain_attn).astype(jnp.bfloat16)
    qkv = jnp.dot(h_one, w_qkv, preferred_element_type=jnp.float32).astype(jnp.bfloat16)
    qkv = qkv.reshape(LEVELS, LATS, LONS, 3 * width)
    query = qkv[..., :width]
    paired = jnp.pad(qkv[..., width:], ((0, 0), (RIM, RIM), (0, 0), (0, 0)))
    paired = jnp.concatenate([paired, paired], axis=2)
    bands = []
    for band in range(LAT_BANDS):
        wide = widths[band].astype(jnp.int32)
        offset = shifts[band].astype(jnp.int32)
        q_band = query[:, band * ROWS:(band + 1) * ROWS]
        k_band = paired[:, band * ROWS:band * ROWS + EXT]
        lat_rows = band * ROWS - RIM + jnp.arange(EXT, dtype=jnp.int32)
        rows_ok = (lat_rows >= 0) & (lat_rows < LATS)
        bias = esb[band * ROWS:(band + 1) * ROWS]

        def one_block(block):
            group = (block - offset) % N_LON // wide
            first = ((offset + group * wide) % N_LON).astype(jnp.int32)
            q_blk = lax.dynamic_slice_in_dim(q_band, (block * COLS).astype(jnp.int32), COLS, 2)
            k_blk = lax.dynamic_slice_in_dim(k_band, (first * COLS).astype(jnp.int32), WMAX * COLS, 2)
            cols_ok = jnp.arange(WMAX * COLS, dtype=jnp.int32) < wide * COLS
            return attend(q_blk, k_blk, bias, rows_ok, cols_ok)
        blocks = lax.map(one_block, jnp.arange(N_LON, dtype=jnp.int32))
        blocks = blocks.reshape(N_LON, LEVELS, ROWS, COLS, width).transpose(1, 2, 0, 3, 4)
        bands.append(blocks.reshape(LEVELS, ROWS, LONS, width))
    attn = jnp.concatenate(bands, axis=1).reshape(-1, width).astype(jnp.bfloat16)
    mixed = (flat + jnp.dot(attn, w_out, preferred_element_type=jnp.float32)).astype(jnp.bfloat16)
    h_two = normalize(mixed.astype(jnp.float32), gain_mlp).astype(jnp.bfloat16)
    hidden = jax.nn.gelu(jnp.dot(h_two, w_up, preferred_element_type=jnp.float32), approximate=False).astype(jnp.bfloat16)
    result = mixed.astype(jnp.float32) + jnp.dot(hidden, w_down, preferred_element_type=jnp.float32)
    return result.astype(jnp.bfloat16).reshape(tokens.shape)
```

```python
import functools
import math

import jax
import jax.numpy as jnp
from jax import lax
from jax.experimental import pallas as pl
from jax.experimental.pallas import tpu as pltpu
from jax.sharding import PartitionSpec as P

EPS = 1e-05
NEG = -1e30
LOW = -3e38
LANES = 128
F32 = jnp.float32
BF16 = jnp.bfloat16
MESH = pl.DeviceIdType.MESH


def normalize(rows, gain):
    mean = jnp.mean(rows, axis=-1, keepdims=True)
    centred = rows - mean
    spread = jnp.mean(centred * centred, axis=-1, keepdims=True)
    return centred * lax.rsqrt(spread + EPS) * gain


def dot(a, b):
    return jnp.dot(a, b, preferred_element_type=F32)


def flip(index, bit):
    return index + bit - 2 * bit * ((index // bit) % 2)


def start_queries(h_one, esb_ref, w_qkv_ref, q_aug, heads, dim, rows):
    count, width = h_one.shape
    per_row = count // rows
    queries = dot(h_one, w_qkv_ref[:, :width]).astype(BF16).astype(F32)
    queries = queries * (dim ** (-0.5) * math.log2(math.e))
    lane = lax.broadcasted_iota(jnp.int32, (per_row, LANES), 1)
    group = LANES // dim
    biases = [bias_lanes(esb_ref[r], dim) for r in range(rows)]
    for h in range(heads):
        at = h // group * LANES
        turn = h % group * dim
        for r in range(rows):
            piece = queries[r * per_row : (r + 1) * per_row, at : at + LANES]
            high = piece.astype(BF16).astype(F32)
            low = piece - high
            if turn:
                high = pltpu.roll(high, LANES - turn, 1)
            if turn != dim:
                low = pltpu.roll(low, (dim - turn) % LANES, 1)
            bias = jnp.broadcast_to(biases[r][h : h + 1, :], (per_row, LANES))
            packed = jnp.where(lane < dim, high, jnp.where(lane < 2 * dim, low, bias))
            q_aug[h, r * per_row : (r + 1) * per_row, :] = packed.astype(BF16)


def start_state(k_aug, v_aug, top, acc, heads, dim, ext, rows):
    span = k_aug.shape[2]
    per_row = LANES
    row = lax.broadcasted_iota(jnp.int32, (16, span), 0)
    key = lax.broadcasted_iota(jnp.int32, (16, span), 1)
    place = (key // per_row + (ext - rows) // 2) % ext
    hot = ((row % ext) == place) & (row < 3 * ext)
    k_aug[:, 2 * dim + 16 :, :] = jnp.zeros((heads, k_aug.shape[1] - 2 * dim - 16, span), BF16)
    v_aug[:, :, LANES:] = jnp.ones((v_aug.shape[0], span, LANES), BF16)
    top[...] = jnp.full(top.shape, LOW, F32)
    acc[...] = jnp.zeros(acc.shape, F32)
    return hot.astype(F32), row


def attend(block, mask, hot, row, w_kt, w_qkv_ref, q_aug, k_aug, v_aug, scores, probs, top, acc, heads, dim):
    span, width = block.shape
    count = q_aug.shape[1]
    group = LANES // dim
    extra = jnp.where(row == 15, jnp.broadcast_to(mask, row.shape), hot).astype(BF16)
    for g in range(width // LANES):
        keys = lax.dot_general(
            w_kt[g * LANES : (g + 1) * LANES, :], block, (((1,), (1,)), ((), ())), preferred_element_type=F32
        ).astype(BF16)
        for j in range(group):
            h = g * group + j
            head = keys[j * dim : (j + 1) * dim, :]
            k_aug[h, :dim, :] = head
            k_aug[h, dim : 2 * dim, :] = head
            k_aug[h, 2 * dim : 2 * dim + 16, :] = extra
    values = dot(block, w_qkv_ref[:, 2 * width :]).astype(BF16)
    for g in range(width // LANES):
        v_aug[g, :, :LANES] = values[:, g * LANES : (g + 1) * LANES]

    def product(h, slot):
        scores[slot][...] = dot(q_aug[h], k_aug[h])

    def soften(h, slot):
        step = 32
        for at in range(0, count, step):
            s = scores[slot][at : at + step, :]
            old = top[h, at : at + step, :]
            new = jnp.maximum(old, jnp.max(s, axis=1, keepdims=True))
            top[h, at : at + step, :] = new
            alpha = jnp.exp2(old - new)
            wide = jnp.concatenate([new] * (span // LANES), axis=1)
            probs[slot][at : at + step, :] = jnp.exp2(s - wide).astype(BF16)
            acc[h, at : at + step, :] = acc[h, at : at + step, :] * jnp.concatenate([alpha, alpha], axis=1)
        acc[h] += dot(probs[slot][...], v_aug[h // group])

    product(0, 0)

    def pair(i, carry):
        product(2 * i + 1, 1)
        soften(2 * i, 0)
        product(jnp.minimum(2 * i + 2, heads - 1), 0)
        soften(2 * i + 1, 1)
        return carry

    lax.fori_loop(0, heads // 2, pair, 0)


def finish(flat, acc, w_out_ref, gain_mlp_ref, w_up_ref, w_down_ref, heads, dim):
    count, width = flat.shape
    group = LANES // dim
    lane = lax.broadcasted_iota(jnp.int32, (count, LANES), 1)
    parts = []
    for g in range(width // LANES):
        part = jnp.zeros((count, LANES), F32)
        for j in range(group):
            h = g * group + j
            part = jnp.where(lane // dim == j, acc[h, :, :LANES] / acc[h, :, LANES:], part)
        parts.append(part.astype(BF16))
    attn = jnp.concatenate(parts, axis=1)
    mixed = (flat.astype(F32) + dot(attn, w_out_ref[...])).astype(BF16)
    h_two = normalize(mixed.astype(F32), gain_mlp_ref[...]).astype(BF16)
    up = dot(h_two, w_up_ref[...])
    hidden = (0.5 * up * (1.0 + lax.erf(up * math.sqrt(0.5)))).astype(BF16)
    return (mixed.astype(F32) + dot(hidden, w_down_ref[...])).astype(BF16)


def by_row(tokens_ref, rows, width):
    return jnp.concatenate([tokens_ref[:, r].reshape(-1, width) for r in range(rows)], axis=0)


def layer_kernel(heads, dim, ext, n_lon, n_lat, remote, *refs):
    tokens_ref, esb_ref, gain_attn_ref, gain_mlp_ref, widths_ref, shifts_ref = refs[:6]
    weights, refs = refs[6:10], refs[10:]
    if remote:
        out_ref, blocks, send, recv = refs[:4]
        refs = refs[4:]
    else:
        blocks, out_ref = refs[:2]
        refs = refs[2:]
    q_aug, k_aug, v_aug, scores_a, scores_b, probs_a, probs_b, top, acc, w_kt = refs[:10]
    w_qkv_ref, w_out_ref, w_up_ref, w_down_ref, loads = refs[10:]
    levels, rows, cols, width = tokens_ref.shape
    per_row = levels * cols
    rim = (ext - rows) // 2
    span = k_aug.shape[2]
    band = lax.axis_index("lat")
    place = lax.axis_index("lon")
    core = place % 2
    other = 1 - core
    fetch = [
        pltpu.make_async_copy(weights[i], (w_qkv_ref, w_out_ref, w_up_ref, w_down_ref)[i], loads.at[i])
        for i in range(4)
    ]
    for copy in fetch:
        copy.start()

    sibling, over_x, over_y = flip(place, 1), flip(place, 2), flip(place, 4)
    has_above, has_below = band < n_lat - 1, band > 0

    if remote:
        barrier = pltpu.get_barrier_semaphore()
        for target in (sibling, over_x, over_y):
            pl.semaphore_signal(barrier, inc=1, device_id={"lon": target}, device_id_type=MESH)

        @pl.when(has_above)
        def _():
            pl.semaphore_signal(barrier, inc=1, device_id={"lat": band + 1}, device_id_type=MESH)

        @pl.when(has_below)
        def _():
            pl.semaphore_signal(barrier, inc=1, device_id={"lat": band - 1}, device_id_type=MESH)

        def remote_copy(at, source, target, device):
            return pltpu.make_async_remote_copy(
                src_ref=source, dst_ref=target, send_sem=send.at[at], recv_sem=recv.at[at],
                device_id=device, device_id_type=MESH,
            )

        own = blocks.at[core]
        centre, frame = pl.ds(0, rows), pl.ds(rows, 2 * rim)
        to_above = remote_copy(0, own.at[pl.ds(rows - rim, rim)], own.at[pl.ds(rows + rim, rim)], {"lat": band + 1})
        to_below = remote_copy(1, own.at[pl.ds(0, rim)], own.at[pl.ds(rows, rim)], {"lat": band - 1})

        def three(first, part):
            return (
                remote_copy(first, own.at[part], own.at[part], {"lon": sibling}),
                remote_copy(first + 1, own.at[part], blocks.at[2 + core].at[part], {"lon": over_x}),
                remote_copy(first + 2, own.at[part], blocks.at[4 + core].at[part], {"lon": over_y}),
            )

        early, late = three(2, centre), three(5, frame)
        from_sibling = [
            remote_copy(at, blocks.at[other].at[part], blocks.at[other].at[part], {"lon": sibling})
            for at, part in ((2, centre), (5, frame))
        ]
        forward = [
            remote_copy(7 + k, blocks.at[2 * k + core], blocks.at[2 * k + core], {"lon": sibling}) for k in (1, 2, 3)
        ]
        arrive = [
            remote_copy(7 + k, blocks.at[2 * k + other], blocks.at[2 * k + other], {"lon": sibling}) for k in (1, 2, 3)
        ]
        across = remote_copy(
            11, blocks.at[4 - core], blocks.at[6 + core], {"lon": place + (over_x - place) * other + (over_y - place) * core}
        )

    flat = by_row(tokens_ref, rows, width)
    h_one = normalize(flat.astype(F32), gain_attn_ref[...]).astype(BF16)

    if remote:
        blocks[core, :rows] = h_one.reshape(rows, levels, cols, width)

        @pl.when(band == n_lat - 1)
        def _():
            blocks[core, rows : rows + rim] = jnp.zeros((rim, levels, cols, width), BF16)

        @pl.when(band == 0)
        def _():
            blocks[core, rows + rim :] = jnp.zeros((rim, levels, cols, width), BF16)

        pl.semaphore_wait(barrier, 3 + jnp.where(has_above, 1, 0) + jnp.where(has_below, 1, 0))
        pl.when(has_above)(to_above.start)
        pl.when(has_below)(to_below.start)
        for copy in early:
            copy.start()
        pl.when(has_above)(to_below.wait_recv)
        pl.when(has_below)(to_above.wait_recv)
        for copy in late:
            copy.start()

    fetch[0].wait()
    start_queries(h_one, esb_ref, w_qkv_ref, q_aug, heads, dim, rows)
    w_kt[...] = w_qkv_ref[:, width : 2 * width].T
    hot, row = start_state(k_aug, v_aug, top, acc, heads, dim, ext, rows)

    wide, offset = widths_ref[band], shifts_ref[band]
    key = lax.broadcasted_iota(jnp.int32, (1, span), 1)
    lat_row = band * rows - rim + (key // per_row + rim) % ext
    row_ok = (lat_row >= 0) & (lat_row < rows * n_lat)
    home = (place - offset) & (n_lon - 1)

    if remote:
        for copy in from_sibling:
            copy.wait_recv()

    def step(s, carry):
        if remote:

            @pl.when(s == 1)
            def _():
                early[1].wait_recv()
                late[1].wait_recv()
                forward[0].start()
                early[2].wait_recv()
                late[2].wait_recv()
                forward[1].start()
                across.start()
                arrive[0].wait_recv()

            @pl.when(s == 2)
            def _():
                arrive[1].wait_recv()
                across.wait_recv()
                forward[2].start()

            @pl.when(s == 3)
            def _():
                arrive[2].wait_recv()

            first = ((place // 2) ^ s) * 2
        else:
            first = 2 * s
        source = first + key // (ext * per_row)
        col_ok = (((source - offset) & (n_lon - 1)) ^ home) < wide
        mask = jnp.where(row_ok & col_ok, 0.0, NEG)
        block = blocks[pl.ds(pl.multiple_of(2 * s, 2), 2)].reshape(span, width)
        attend(
            block, mask, hot, row, w_kt, w_qkv_ref, q_aug, k_aug, v_aug,
            (scores_a, scores_b), (probs_a, probs_b), top, acc, heads, dim,
        )
        return carry

    lax.fori_loop(0, n_lon // 2, step, 0)
    for copy in fetch[1:]:
        copy.wait()
    flat = by_row(tokens_ref, rows, width)
    result = finish(flat, acc, w_out_ref, gain_mlp_ref, w_up_ref, w_down_ref, heads, dim)
    for r in range(rows):
        out_ref[:, r] = result[r * per_row : (r + 1) * per_row].reshape(levels, cols, width)
    if remote:
        pl.when(has_above)(to_above.wait_send)
        pl.when(has_below)(to_below.wait_send)
        for copy in (*early, *late, *forward, across):
            copy.wait_send()


def work_buffers(heads, count, width, span):
    return [
        pltpu.VMEM((heads, count, LANES), BF16),
        pltpu.VMEM((heads, LANES, span), BF16),
        pltpu.VMEM((width // LANES, span, 2 * LANES), BF16),
        pltpu.VMEM((count, span), F32),
        pltpu.VMEM((count, span), F32),
        pltpu.VMEM((count, span), BF16),
        pltpu.VMEM((count, span), BF16),
        pltpu.VMEM((heads, count, LANES), F32),
        pltpu.VMEM((heads, count, 2 * LANES), F32),
        pltpu.VMEM((width, width), BF16),
    ]


def bias_lanes(esb, dim):
    heads, ext = esb.shape
    lane = lax.broadcasted_iota(jnp.int32, (heads, LANES), 1) - 2 * dim
    used = (lane >= 0) & (lane < 3 * ext)
    bias = jnp.zeros((heads, LANES), F32)
    for e in range(ext):
        here = used & (lane % ext == e)
        bias = jnp.where(here, jnp.broadcast_to(esb[:, e : e + 1], (heads, LANES)), bias)
    bias = bias * math.log2(math.e)
    high = bias.astype(BF16).astype(F32)
    middle = (bias - high).astype(BF16).astype(F32)
    low = bias - high - middle
    pieces = jnp.where(lane < ext, high, jnp.where(lane < 2 * ext, middle, low))
    return jnp.where(lane == 3 * ext, 1.0, pieces)


def shards(tokens, gain_attn, w_qkv, esb, w_out, gain_mlp, w_up, w_down, widths, shifts):
    levels, rows, cols, width = tokens.shape
    heads, ext = esb.shape[1:]
    rim = (ext - rows) // 2
    dim = width // heads
    n_lon = lax.axis_size("lon")
    n_lat = lax.axis_size("lat")
    per_row = levels * cols
    span = 2 * ext * per_row
    remote = n_lon == 8
    operands = [tokens, esb, gain_attn, gain_mlp, widths, shifts, w_qkv, w_out, w_up, w_down]
    vmem = pl.BlockSpec(memory_space=pltpu.VMEM)
    smem = pl.BlockSpec(memory_space=pltpu.SMEM)
    specs = [vmem] * 4 + [smem] * 2 + [pl.BlockSpec(memory_space=pl.ANY)] * 4
    scratch = work_buffers(heads, rows * per_row, width, span)
    scratch += [pltpu.VMEM(w.shape, BF16) for w in operands[6:]] + [pltpu.SemaphoreType.DMA((4,))]
    params = dict(vmem_limit_bytes=58 * 1024 * 1024)
    if remote:
        scratch = [
            pltpu.VMEM((n_lon, ext, levels, cols, width), BF16),
            pltpu.SemaphoreType.DMA((12,)),
            pltpu.SemaphoreType.DMA((12,)),
        ] + scratch
        params.update(collective_id=0, has_side_effects=True)
    else:
        h_one = normalize(tokens.astype(F32), gain_attn).astype(BF16).transpose(1, 0, 2, 3)
        up = [(i, i + 1) for i in range(n_lat - 1)]
        down = [(i + 1, i) for i in range(n_lat - 1)]
        framed = jnp.concatenate(
            [h_one, lax.ppermute(h_one[:rim], "lat", down), lax.ppermute(h_one[rows - rim :], "lat", up)], axis=0
        )
        operands.append(lax.all_gather(framed, "lon", axis=0, tiled=False))
        specs.append(vmem)
    return pl.pallas_call(
        functools.partial(layer_kernel, heads, dim, ext, n_lon, n_lat, remote),
        out_shape=jax.ShapeDtypeStruct(tokens.shape, BF16),
        in_specs=specs,
        out_specs=vmem,
        scratch_shapes=scratch,
        compiler_params=pltpu.CompilerParams(**params),
    )(*operands)


def solution(mesh):
    placed = (P(None, "lat", "lon", None), P(), P(), P("lat", None, None), P(), P(), P(), P(), P(), P())
    return jax.shard_map(
        shards, mesh=mesh, in_specs=placed, out_specs=P(None, "lat", "lon", None), check_vma=False
    )
```

```python
import functools
import math

import jax
import jax.numpy as jnp
from jax import lax
from jax.experimental import pallas as pl
from jax.experimental.pallas import tpu as pltpu
from jax.sharding import PartitionSpec as P

EPS = 1e-05
NEG = -1e30
LOW = -3e38
LANES = 128
F32 = jnp.float32
BF16 = jnp.bfloat16
MESH = pl.DeviceIdType.MESH


def normalize(rows, gain):
    mean = jnp.mean(rows, axis=-1, keepdims=True)
    centred = rows - mean
    spread = jnp.mean(centred * centred, axis=-1, keepdims=True)
    return centred * lax.rsqrt(spread + EPS) * gain


def dot(a, b):
    return jnp.dot(a, b, preferred_element_type=F32)


def flip(index, bit):
    return index + bit - 2 * bit * ((index // bit) % 2)


def start_queries(h_one, esb_ref, w_qkv_ref, q_aug, heads, dim, rows):
    count, width = h_one.shape
    per_row = count // rows
    queries = dot(h_one, w_qkv_ref[:, :width]).astype(BF16).astype(F32)
    queries = queries * (dim ** (-0.5) * math.log2(math.e))
    lane = lax.broadcasted_iota(jnp.int32, (per_row, LANES), 1)
    group = LANES // dim
    biases = [bias_lanes(esb_ref[r], dim) for r in range(rows)]
    for h in range(heads):
        at = h // group * LANES
        turn = h % group * dim
        for r in range(rows):
            piece = queries[r * per_row : (r + 1) * per_row, at : at + LANES]
            high = piece.astype(BF16).astype(F32)
            low = piece - high
            if turn:
                high = pltpu.roll(high, LANES - turn, 1)
            if turn != dim:
                low = pltpu.roll(low, (dim - turn) % LANES, 1)
            bias = jnp.broadcast_to(biases[r][h : h + 1, :], (per_row, LANES))
            packed = jnp.where(lane < dim, high, jnp.where(lane < 2 * dim, low, bias))
            q_aug[h, r * per_row : (r + 1) * per_row, :] = packed.astype(BF16)


def start_state(k_aug, v_aug, top, acc, heads, dim):
    span = k_aug.shape[2]
    k_aug[:, 2 * dim + 16 :, :] = jnp.zeros((heads, k_aug.shape[1] - 2 * dim - 16, span), BF16)
    v_aug[:, :, LANES:] = jnp.ones((v_aug.shape[0], span, LANES), BF16)
    top[...] = jnp.full(top.shape, LOW, F32)
    acc[...] = jnp.zeros(acc.shape, F32)


def attend(block, mask, window_row, w_kt, w_qkv_ref, work, heads, dim, ext, between=None):
    q_aug, k_aug, v_aug, scores, probs, alphas, top, acc = work
    span, width = block.shape
    count = q_aug.shape[1]
    group = LANES // dim
    row = lax.broadcasted_iota(jnp.int32, (16, span), 0)
    hot = jnp.where((row % ext == window_row) & (row < 3 * ext), 1.0, 0.0)
    extra = jnp.where(row == 15, jnp.broadcast_to(mask, row.shape), hot).astype(BF16)
    for g in range(width // LANES):
        keys = lax.dot_general(
            w_kt[g * LANES : (g + 1) * LANES, :], block, (((1,), (1,)), ((), ())), preferred_element_type=F32
        ).astype(BF16)
        for j in range(group):
            h = g * group + j
            head = keys[j * dim : (j + 1) * dim, :]
            k_aug[h, :dim, :span] = head
            k_aug[h, dim : 2 * dim, :span] = head
            k_aug[h, 2 * dim : 2 * dim + 16, :span] = extra
    values = dot(block, w_qkv_ref[:, 2 * width :])
    for g in range(width // LANES):
        v_aug[g, :span, :LANES] = values[:, g * LANES : (g + 1) * LANES].astype(BF16)

    def product(h, slot):
        scores[slot][:, :span] = dot(q_aug[h], k_aug[h, :, :span])

    def soften(h, slot):
        step = 32
        for at in range(0, count, step):
            s = scores[slot][at : at + step, :span]
            old = top[h, at : at + step, :]
            new = jnp.maximum(old, jnp.max(s, axis=1, keepdims=True))
            top[h, at : at + step, :] = new
            alphas[slot][at : at + step, :] = jnp.exp2(old - new)
            wide = jnp.concatenate([new] * (span // LANES), axis=1)
            probs[slot][at : at + step, :span] = jnp.exp2(s - wide).astype(BF16)
        fade = jnp.concatenate([alphas[slot][...]] * 2, axis=1)
        acc[h] = acc[h] * fade + dot(probs[slot][:, :span], v_aug[h // group, :span, :])

    product(0, 0)

    def pair(i, carry):
        if between is not None:
            between(i)
        product(2 * i + 1, 1)
        soften(2 * i, 0)
        product(jnp.minimum(2 * i + 2, heads - 1), 0)
        soften(2 * i + 1, 1)
        return carry

    lax.fori_loop(0, heads // 2, pair, 0)


def finish(flat, acc, w_out_ref, gain_mlp_ref, w_up_ref, w_down_ref, heads, dim):
    count, width = flat.shape
    group = LANES // dim
    lane = lax.broadcasted_iota(jnp.int32, (count, LANES), 1)
    parts = []
    for g in range(width // LANES):
        part = jnp.zeros((count, LANES), F32)
        for j in range(group):
            h = g * group + j
            part = jnp.where(lane // dim == j, acc[h, :, :LANES] / acc[h, :, LANES:], part)
        parts.append(part.astype(BF16))
    attn = jnp.concatenate(parts, axis=1)
    mixed = (flat.astype(F32) + dot(attn, w_out_ref[...])).astype(BF16)
    h_two = normalize(mixed.astype(F32), gain_mlp_ref[...]).astype(BF16)
    up = dot(h_two, w_up_ref[...])
    hidden = (0.5 * up * (1.0 + lax.erf(up * math.sqrt(0.5)))).astype(BF16)
    return (mixed.astype(F32) + dot(hidden, w_down_ref[...])).astype(BF16)


def by_row(tokens_ref, rows, width):
    return jnp.concatenate([tokens_ref[:, r].reshape(-1, width) for r in range(rows)], axis=0)


def layer_kernel(heads, dim, ext, n_lon, n_lat, remote, *refs):
    tokens_ref, esb_ref, gain_attn_ref, gain_mlp_ref, widths_ref, shifts_ref = refs[:6]
    weights, refs = refs[6:10], refs[10:]
    if remote:
        out_ref, blocks, send, recv = refs[:4]
        refs = refs[4:]
    else:
        blocks, out_ref = refs[:2]
        refs = refs[2:]
    q_aug, k_aug, v_aug, scores_a, scores_b, probs_a, probs_b, alpha_a, alpha_b, top, acc, w_kt = refs[:12]
    w_qkv_ref, w_out_ref, w_up_ref, w_down_ref, loads = refs[12:]
    levels, rows, cols, width = tokens_ref.shape
    per_row = levels * cols
    rim = (ext - rows) // 2
    work = (q_aug, k_aug, v_aug, (scores_a, scores_b), (probs_a, probs_b), (alpha_a, alpha_b), top, acc)
    band = lax.axis_index("lat")
    place = lax.axis_index("lon")
    core = place % 2
    other = 1 - core
    fetch = [
        pltpu.make_async_copy(weights[i], (w_qkv_ref, w_out_ref, w_up_ref, w_down_ref)[i], loads.at[i])
        for i in range(4)
    ]
    for copy in fetch:
        copy.start()

    sibling, over_x, over_y = flip(place, 1), flip(place, 2), flip(place, 4)
    has_above, has_below = band < n_lat - 1, band > 0

    if remote:
        barrier = pltpu.get_barrier_semaphore()
        for target in (sibling, over_x, over_y):
            pl.semaphore_signal(barrier, inc=1, device_id={"lon": target}, device_id_type=MESH)

        @pl.when(has_above)
        def _():
            pl.semaphore_signal(barrier, inc=1, device_id={"lat": band + 1}, device_id_type=MESH)

        @pl.when(has_below)
        def _():
            pl.semaphore_signal(barrier, inc=1, device_id={"lat": band - 1}, device_id_type=MESH)

        def remote_copy(at, source, target, device):
            return pltpu.make_async_remote_copy(
                src_ref=source, dst_ref=target, send_sem=send.at[at], recv_sem=recv.at[at],
                device_id=device, device_id_type=MESH,
            )

        own = blocks.at[core]
        centre, frame = pl.ds(0, rows), pl.ds(rows, 2 * rim)
        to_above = remote_copy(0, own.at[pl.ds(rows - rim, rim)], own.at[pl.ds(rows + rim, rim)], {"lat": band + 1})
        to_below = remote_copy(1, own.at[pl.ds(0, rim)], own.at[pl.ds(rows, rim)], {"lat": band - 1})

        def three(first, part):
            return (
                remote_copy(first, own.at[part], own.at[part], {"lon": sibling}),
                remote_copy(first + 1, own.at[part], blocks.at[2 + core].at[part], {"lon": over_x}),
                remote_copy(first + 2, own.at[part], blocks.at[4 + core].at[part], {"lon": over_y}),
            )

        early, late = three(2, centre), three(5, frame)
        from_sibling = [
            remote_copy(at, blocks.at[other].at[part], blocks.at[other].at[part], {"lon": sibling})
            for at, part in ((2, centre), (5, frame))
        ]
        whole = pl.ds(0, ext)
        passed = ((8, 1, centre), (9, 2, centre), (10, 1, frame), (11, 2, frame), (12, 3, whole))
        forward = [
            remote_copy(at, blocks.at[2 * k + core].at[part], blocks.at[2 * k + core].at[part], {"lon": sibling})
            for at, k, part in passed
        ]
        arrive = [
            remote_copy(at, blocks.at[2 * k + other].at[part], blocks.at[2 * k + other].at[part], {"lon": sibling})
            for at, k, part in passed
        ]
        across = remote_copy(
            13, blocks.at[4 - core], blocks.at[6 + core], {"lon": place + (over_x - place) * other + (over_y - place) * core}
        )

    flat = by_row(tokens_ref, rows, width)
    h_one = normalize(flat.astype(F32), gain_attn_ref[...]).astype(BF16)

    if remote:
        blocks[core, :rows] = h_one.reshape(rows, levels, cols, width)

        @pl.when(band == n_lat - 1)
        def _():
            blocks[core, rows : rows + rim] = jnp.zeros((rim, levels, cols, width), BF16)

        @pl.when(band == 0)
        def _():
            blocks[core, rows + rim :] = jnp.zeros((rim, levels, cols, width), BF16)

        pl.semaphore_wait(barrier, 3 + jnp.where(has_above, 1, 0) + jnp.where(has_below, 1, 0))
        pl.when(has_above)(to_above.start)
        pl.when(has_below)(to_below.start)
        for copy in early:
            copy.start()

    fetch[0].wait()
    start_queries(h_one, esb_ref, w_qkv_ref, q_aug, heads, dim, rows)
    w_kt[...] = w_qkv_ref[:, width : 2 * width].T
    start_state(k_aug, v_aug, top, acc, heads, dim)

    wide, offset = widths_ref[band], shifts_ref[band]
    home = (place - offset) & (n_lon - 1)

    def describe(pieces):
        masks, lines, parts = [], [], []
        for pair, at, lines_in in pieces:
            here = lines_in * per_row
            key = lax.broadcasted_iota(jnp.int32, (1, 2 * here), 1)
            line = (at + (key % here) // per_row + rim) % ext
            first = ((place // 2) ^ pair) * 2 if remote else 2 * pair
            source = first + key // here
            lat_row = band * rows - rim + line
            row_ok = (lat_row >= 0) & (lat_row < rows * n_lat)
            col_ok = (((source - offset) & (n_lon - 1)) ^ home) < wide
            masks.append(jnp.where(row_ok & col_ok, 0.0, NEG))
            lines.append(line)
            tokens = blocks[pl.ds(pl.multiple_of(2 * pair, 2), 2), at : at + lines_in]
            parts.append(tokens.reshape(2 * here, width))
        join = lambda x, axis: jnp.concatenate(x, axis=axis) if len(x) > 1 else x[0]
        return join(parts, 0), join(masks, 1), join(lines, 1)

    def centres(s, between=None):
        attend(*describe([(s, 0, rows)]), w_kt, w_qkv_ref, work, heads, dim, ext, between)

    def rest(s, between=None):
        a = 2 * (s - n_pairs // 2)
        pieces = [(a, rows, 2 * rim), (a + 1, rows, 2 * rim), (s, 0, rows)]
        attend(*describe(pieces), w_kt, w_qkv_ref, work, heads, dim, ext, between)

    n_pairs = n_lon // 2
    if remote:
        from_sibling[0].wait_recv()

    def first_half(s, carry):
        def between(i):
            rim_time = (s == 0) & (i == 1)
            pl.when(rim_time & has_above)(to_below.wait_recv)
            pl.when(rim_time & has_below)(to_above.wait_recv)

            @pl.when(rim_time)
            def _():
                for copy in late:
                    copy.start()

            @pl.when((s == 1) & (i == 3))
            def _():
                early[2].wait_recv()
                forward[1].start()
                late[1].wait_recv()
                forward[2].start()
                late[2].wait_recv()
                forward[3].start()
                across.start()

        if remote:

            @pl.when(s == 1)
            def _():
                early[1].wait_recv()
                forward[0].start()
                arrive[0].wait_recv()

        centres(s, between if remote else None)
        return carry

    def second_half(s, carry):
        def between(i):
            @pl.when((s == 2) & (i == 4))
            def _():
                across.wait_recv()
                forward[4].start()

        if remote:

            @pl.when(s == 2)
            def _():
                from_sibling[1].wait_recv()
                arrive[1].wait_recv()
                arrive[2].wait_recv()
                arrive[3].wait_recv()

            @pl.when(s == 3)
            def _():
                arrive[4].wait_recv()

        rest(s, between if remote else None)
        return carry

    lax.fori_loop(0, n_pairs // 2, first_half, 0)
    lax.fori_loop(n_pairs // 2, n_pairs, second_half, 0)
    for copy in fetch[1:]:
        copy.wait()
    flat = by_row(tokens_ref, rows, width)
    result = finish(flat, acc, w_out_ref, gain_mlp_ref, w_up_ref, w_down_ref, heads, dim)
    for r in range(rows):
        out_ref[:, r] = result[r * per_row : (r + 1) * per_row].reshape(levels, cols, width)
    if remote:
        pl.when(has_above)(to_above.wait_send)
        pl.when(has_below)(to_below.wait_send)
        for copy in (*early, *late, *forward, across):
            copy.wait_send()


def work_buffers(heads, count, width, span):
    return [
        pltpu.VMEM((heads, count, LANES), BF16),
        pltpu.VMEM((heads, LANES, span), BF16),
        pltpu.VMEM((width // LANES, span, 2 * LANES), BF16),
        pltpu.VMEM((count, span), F32),
        pltpu.VMEM((count, span), F32),
        pltpu.VMEM((count, span), BF16),
        pltpu.VMEM((count, span), BF16),
        pltpu.VMEM((count, LANES), F32),
        pltpu.VMEM((count, LANES), F32),
        pltpu.VMEM((heads, count, LANES), F32),
        pltpu.VMEM((heads, count, 2 * LANES), F32),
        pltpu.VMEM((width, width), BF16),
    ]


def bias_lanes(esb, dim):
    heads, ext = esb.shape
    lane = lax.broadcasted_iota(jnp.int32, (heads, LANES), 1) - 2 * dim
    used = (lane >= 0) & (lane < 3 * ext)
    bias = jnp.zeros((heads, LANES), F32)
    for e in range(ext):
        here = used & (lane % ext == e)
        bias = jnp.where(here, jnp.broadcast_to(esb[:, e : e + 1], (heads, LANES)), bias)
    bias = bias * math.log2(math.e)
    high = bias.astype(BF16).astype(F32)
    middle = (bias - high).astype(BF16).astype(F32)
    low = bias - high - middle
    pieces = jnp.where(lane < ext, high, jnp.where(lane < 2 * ext, middle, low))
    return jnp.where(lane == 3 * ext, 1.0, pieces)


def shards(tokens, gain_attn, w_qkv, esb, w_out, gain_mlp, w_up, w_down, widths, shifts):
    levels, rows, cols, width = tokens.shape
    heads, ext = esb.shape[1:]
    rim = (ext - rows) // 2
    dim = width // heads
    n_lon = lax.axis_size("lon")
    n_lat = lax.axis_size("lat")
    per_row = levels * cols
    span = 2 * (rows + 4 * rim) * per_row
    remote = n_lon == 8
    operands = [tokens, esb, gain_attn, gain_mlp, widths, shifts, w_qkv, w_out, w_up, w_down]
    vmem = pl.BlockSpec(memory_space=pltpu.VMEM)
    smem = pl.BlockSpec(memory_space=pltpu.SMEM)
    specs = [vmem] * 4 + [smem] * 2 + [pl.BlockSpec(memory_space=pl.ANY)] * 4
    scratch = work_buffers(heads, rows * per_row, width, span)
    scratch += [pltpu.VMEM(w.shape, BF16) for w in operands[6:]] + [pltpu.SemaphoreType.DMA((4,))]
    params = dict(vmem_limit_bytes=58 * 1024 * 1024)
    if remote:
        scratch = [
            pltpu.VMEM((n_lon, ext, levels, cols, width), BF16),
            pltpu.SemaphoreType.DMA((14,)),
            pltpu.SemaphoreType.DMA((14,)),
        ] + scratch
        params.update(collective_id=0, has_side_effects=True)
    else:
        h_one = normalize(tokens.astype(F32), gain_attn).astype(BF16).transpose(1, 0, 2, 3)
        up = [(i, i + 1) for i in range(n_lat - 1)]
        down = [(i + 1, i) for i in range(n_lat - 1)]
        framed = jnp.concatenate(
            [h_one, lax.ppermute(h_one[:rim], "lat", down), lax.ppermute(h_one[rows - rim :], "lat", up)], axis=0
        )
        operands.append(lax.all_gather(framed, "lon", axis=0, tiled=False))
        specs.append(vmem)
    return pl.pallas_call(
        functools.partial(layer_kernel, heads, dim, ext, n_lon, n_lat, remote),
        out_shape=jax.ShapeDtypeStruct(tokens.shape, BF16),
        in_specs=specs,
        out_specs=vmem,
        scratch_shapes=scratch,
        compiler_params=pltpu.CompilerParams(**params),
    )(*operands)


def solution(mesh):
    placed = (P(None, "lat", "lon", None), P(), P(), P("lat", None, None), P(), P(), P(), P(), P(), P())
    return jax.shard_map(
        shards, mesh=mesh, in_specs=placed, out_specs=P(None, "lat", "lon", None), check_vma=False
    )
```
